256 devices in a mesh: prow: 16 (over x_hi, z), pcol: 16 (over y, x_lo, core).
Axes of the slice: x: 4 (x_hi: 2, x_lo: 2; x = x_hi * 2 + x_lo), y: 4, z: 8, core: 2. Of those that a mesh axis runs over, the one named last changes fastest.
Arguments:
- ancestor_inverse: float32 [10, 16, 128, 10, 16, 128], P(None, 'prow', None, None, 'pcol'), may hold values from -6 to 6
- factor_panel: float32 [2, 10, 16, 128, 256], P(None, None, 'prow'), may hold values from -0.046875 to 0.046875
- structure: int32 [2, 120], replicated, may hold values from 0 to 159, as said below
- block_map: int32 [160], replicated, may hold values from 0 to 159, each once
- diag_inverse: float32 [2, 256, 256], replicated, may hold values from -6 to 6
Outputs:
- ancestor_columns: float32 [2, 16, 16, 80, 256], P(None, 'prow', 'pcol')
- diag_block: float32 [2, 256, 256], replicated
The draws below stay inside these ranges and needn't reach their ends.
Inputs may be any that keep to these rules, and one draw needn't show every extreme that they name: `structure`: each row lists 120 different ancestor blocks in increasing order; the first is block 0 and the last is block 159 in every row.
All inputs are finite; a program needn't handle non-finite values.
Results may differ from the reference program's by a relative error of at most 0.00007.
Values sent between devices are 32-bit elements; how exact they have to be, the bound alone decides.
A program may use at most 128 MiB of HBM per device.

```python
import jax
import jax.numpy as jnp
from jax import lax

W = 256
BS = 128
ROW_BLK = 10
NB = 160
CB = 10
SB = 120
ORDER = 20480
SHARE = 80
N_PROW = 16
N_PCOL = 16


def draw_structure(key, part):
    key = jax.random.fold_in(key, 7)
    chosen_rows = []
    for group_member in range(2):
        chosen = (jax.random.permutation(jax.random.fold_in(key, group_member), NB - 2)[:SB - 2] + 1).astype(jnp.int32)
        joined = jnp.concatenate([jnp.array([0], jnp.int32), chosen, jnp.array([NB - 1], jnp.int32)])
        chosen_rows.append(jnp.sort(joined))
    return jnp.stack(chosen_rows)


def block_levels(own_key, dims, cuts, low, largest):
    loudness, own = 1.0, jax.random.fold_in(own_key, 6)
    for axis_at, blocks in cuts:
        steps = jnp.exp(jax.random.uniform(jax.random.fold_in(own, axis_at), (blocks,), jnp.float32, low / len(cuts), largest / len(cuts)))
        loudness = loudness * jnp.repeat(steps, dims[axis_at] // blocks).reshape([-1 if axis == axis_at else 1 for axis in range(len(dims))])
    return loudness


def bell_draw(rng, extent, scale, most, split=(), kind=jnp.bfloat16):
    values = scale * jax.random.normal(rng, extent, jnp.float32)
    if split:
        values = values * block_levels(rng, extent, split, -0.22, 0.18)
    return jnp.clip(values, -most, most).astype(kind)


def setup_inputs(seed: int = 0) -> dict:
    streams_of = jax.random.split(jax.random.key(seed), 6)
    return {
        "ancestor_inverse": bell_draw(streams_of[0], (ROW_BLK, N_PROW, BS, CB, N_PCOL, BS), 1.0, 6.0, ((1, 16), (4, 16)), jnp.float32),
        "factor_panel": bell_draw(streams_of[1], (2, ROW_BLK, N_PROW, BS, W), (SB * BS) ** -0.5, 0.046875, ((2, 16),), jnp.float32),
        "structure": draw_structure(jax.random.fold_in(streams_of[5], 71), 0),
        "block_map": jax.random.permutation(streams_of[3], NB).astype(jnp.int32),
        "diag_inverse": bell_draw(streams_of[4], (2, W, W), 1.0, 6.0, (), jnp.float32),
    }


def reference(ancestor_inverse, factor_panel, structure, block_map, diag_inverse):
    matrix = ancestor_inverse.reshape(ORDER, ORDER)
    slot_ids = block_map[structure]
    live_mask = jnp.any(slot_ids[:, :, None] == jnp.arange(NB, dtype=jnp.int32)[None, None, :], axis=1).astype(jnp.float32)
    rows_live = jnp.repeat(live_mask, BS, axis=1)
    masked_panel = factor_panel.reshape(2, ORDER, W) * rows_live[:, :, None]
    stacked = jnp.transpose(masked_panel, (1, 0, 2)).reshape(ORDER, 2 * W)
    product = jnp.dot(matrix, stacked, precision=lax.Precision.HIGHEST, preferred_element_type=jnp.float32)
    column_list = -jnp.transpose(product.reshape(ORDER, 2, W), (1, 0, 2)) * rows_live[:, :, None]
    diagonal = diag_inverse - jnp.einsum("ksw,ksv->kwv", masked_panel, column_list, precision=lax.Precision.HIGHEST)
    arranged = column_list.reshape(2, ROW_BLK, N_PROW, BS, W).transpose(0, 2, 1, 3, 4).reshape(2, N_PROW, N_PCOL, SHARE, W)
    return arranged, diagonal
```

```python
import functools

import jax
import jax.numpy as jnp
from jax import lax
from jax.experimental import pallas as pl
from jax.experimental.pallas import tpu as pltpu
from jax.sharding import PartitionSpec as P

MESH = pl.DeviceIdType.MESH
F32 = jnp.float32
BF16 = jnp.bfloat16

RING = 8
SUBS = 2
ROWS = 64 // SUBS
STEPS = 2 * 10 * SUBS
LAG = 3
WAIT_A = 8
SHARED = True


def split(value):
    high = value.astype(BF16)
    return high, (value - high.astype(F32)).astype(BF16)


def three_dots(a_high, a_low, b_high, b_low):
    dot = functools.partial(jnp.dot, preferred_element_type=F32)
    return dot(a_high, b_high) + (dot(a_high, b_low) + dot(a_low, b_high))


def kernel(
    live_own, live_col, a_hbm, panel_hbm,
    y_out, d_out,
    a_raw, a_high, a_low, own, own_high, own_low, x, x_high, x_low,
    y, y_peer, y_send, y_recv, d_part, d_peer, d_send, d_recv, d_pair, d_ring,
    load_sem, z_ssem, z_rsem, x_ssem, x_rsem, c_ssem, c_rsem, y_ssem, y_rsem, d_ssem, d_rsem, p_ssem, p_rsem,
    r_ssem, r_rsem, g_ssem, g_rsem,
):
    p = lax.axis_index("prow")
    q = lax.axis_index("pcol")
    half = p // RING
    z = p % RING
    place = q // 2
    core = q % 2
    root_half = q // RING
    hops = (z - q % RING + RING) % RING
    on_root = half == root_half

    across = ((1 - half) * RING + z, q)
    sibling = (p, place * 2 + 1 - core)

    def ring(step):
        return (half * RING + (z + step) % RING, q)

    def chip(step):
        return (p, ((place + step) % 8) * 2 + core)

    load_own = pltpu.make_async_copy(panel_hbm, own, load_sem.at[0])
    load_own.start()
    load_root = pltpu.make_async_copy(panel_hbm, x, load_sem.at[1])

    @pl.when(p == q)
    def _():
        load_root.start()

    load_a = pltpu.make_async_copy(a_hbm, a_raw, load_sem.at[2])
    load_a.start()

    barrier = pltpu.get_barrier_semaphore()
    partners = [across, sibling] + [ring(i) for i in range(1, RING)] + [chip(i) for i in range(1, 8)]
    for partner in partners:
        pl.semaphore_signal(barrier, inc=1, device_id=partner, device_id_type=MESH)
    pl.semaphore_wait(barrier, len(partners))

    @pl.when(p == q)
    def _():
        load_root.wait()

    def chunk(way, s):
        block = s // SUBS
        row = way * 64 + (s % SUBS) * ROWS
        return x.at[block // 10, block % 10, pl.ds(row, ROWS)]

    def z_copy(way, s):
        return pltpu.make_async_remote_copy(
            src_ref=chunk(way, s), dst_ref=chunk(way, s), send_sem=z_ssem.at[way, s], recv_sem=z_rsem.at[way, s],
            device_id=ring(1 if way == 0 else RING - 1), device_id_type=MESH,
        )

    def x_copy(way, s):
        return pltpu.make_async_remote_copy(
            src_ref=chunk(way, s), dst_ref=chunk(way, s), send_sem=x_ssem.at[way, s], recv_sem=x_rsem.at[way, s],
            device_id=across, device_id_type=MESH,
        )

    def roles(way, s):
        if SHARED:
            kind = s % 3
            both = kind == 2
            carries = both | (on_root & (kind == 0)) | (jnp.logical_not(on_root) & (kind == 1))
        else:
            both = jnp.bool_(True)
            carries = jnp.bool_(True)
        done = hops if way == 0 else (RING - hops) % RING
        to_z = carries & (done < RING - 1)
        to_x = jnp.where(hops == 0, on_root, carries & jnp.logical_not(both))
        return carries, to_z, to_x

    def event(way, s):
        carries, to_z, to_x = roles(way, s)

        @pl.when((hops == 0) & jnp.logical_not(on_root))
        def _():
            x_copy(way, s).wait_recv()

        @pl.when((hops != 0) & carries)
        def _():
            z_copy(way, s).wait_recv()

        @pl.when(to_z)
        def _():
            z_copy(way, s).start()

        @pl.when(to_x)
        def _():
            x_copy(way, s).start()

    shift = jnp.where(hops == 0, 0, (RING - 2 * hops) * LAG)
    late_up = jnp.maximum(0, -shift)
    late_down = jnp.maximum(0, shift)

    def split_a(i):
        for col in range(10):
            high, low = split(a_raw[pl.ds(i * 320 + col, 32, stride=10), :])
            rows = pl.ds(pl.multiple_of(i * 32, 32), 32)
            a_high[rows, col * 128 : (col + 1) * 128] = high
            a_low[rows, col * 128 : (col + 1) * 128] = low

    def stream(t, carry):
        for way, late in ((0, late_up), (1, late_down)):
            s = t - late

            @pl.when((s >= 0) & (s < STEPS))
            def _():
                event(way, s)

        @pl.when(t == WAIT_A)
        def _():
            load_a.wait()

        @pl.when((t >= WAIT_A) & (t < WAIT_A + 40))
        def _():
            split_a(t - WAIT_A)

        return carry

    lax.fori_loop(0, max(STEPS + 6 * LAG, WAIT_A + 40), stream, 0)

    load_own.wait()

    def arrived(s, carry):
        for way in range(2):
            carries, _, _ = roles(way, s)

            @pl.when((hops != 0) & jnp.logical_not(carries))
            def _():
                x_copy(way, s).wait_recv()

        return carry

    if SHARED:
        lax.fori_loop(0, STEPS, arrived, 0)

    for k in range(2):

        def to_bf16(r, carry):
            rows = pl.ds(pl.multiple_of(r * 128, 128), 128)
            high, low = split(x[k, r] * live_col[k, r])
            x_high[rows] = high
            x_low[rows] = low
            high, low = split((own[k, r] * live_own[k, r]).T)
            own_high[:, rows] = high
            own_low[:, rows] = low
            return carry

        lax.fori_loop(0, 10, to_bf16, 0)

        def rows_of_y(m, carry):
            rows = pl.ds(pl.multiple_of(m * 160, 32), 160)
            part = three_dots(a_high[rows], a_low[rows], x_high[...], x_low[...])
            y[k, m] = part.reshape(2, 80, 256)
            return carry

        lax.fori_loop(0, 8, rows_of_y, 0)
        y_high, y_low = split(y[k].reshape(1280, 256))
        d_part[k] = three_dots(own_high[...], own_low[...], y_high, y_low).reshape(8, 32, 256)

    def remote(src, dst, send, recv, device):
        return pltpu.make_async_remote_copy(
            src_ref=src, dst_ref=dst, send_sem=send, recv_sem=recv, device_id=device, device_id_type=MESH
        )

    peer_d = remote(d_part.at[1 - core], d_peer, c_ssem.at[0], c_rsem.at[0], sibling)
    peer_y = remote(y.at[:, :, 1 - core], y_peer, c_ssem.at[1], c_rsem.at[1], sibling)
    peer_d.start()
    peer_y.start()
    peer_d.wait()
    for i in range(8):
        d_send[i] = d_part[core, i] + d_peer[i]
    d_copies = []
    for step in range(1, 8):
        to = (place + step) % 8
        copy = remote(d_send.at[to], d_recv.at[place], d_ssem.at[step], d_rsem.at[step], chip(step))
        copy.start()
        d_copies.append(copy)
    peer_y.wait()
    for i in range(8):
        for k in range(2):
            y_send[i, k] = y[k, i, core] + y_peer[k, i]
    y_copies = []
    for step in range(1, 8):
        to = (place + step) % 8
        copy = remote(y_send.at[to], y_recv.at[place], y_ssem.at[step], y_rsem.at[step], chip(step))
        copy.start()
        y_copies.append(copy)

    d_recv[place] = d_send[place]
    for copy in d_copies:
        copy.wait()
    total = d_recv[0]
    for i in range(1, 8):
        total = total + d_recv[i]
    d_pair[0] = total
    pair = remote(d_pair.at[0], d_pair.at[1], p_ssem, p_rsem, across)
    pair.start()
    pair.wait()
    d_ring[z] = d_pair[0] + d_pair[1]
    r_copies = []
    for step in range(1, RING):
        copy = remote(d_ring.at[z], d_ring.at[z], r_ssem.at[step], r_rsem.at[step], ring(step))
        copy.start()
        r_copies.append(copy)

    y_recv[place] = y_send[place]
    for copy in y_copies:
        copy.wait()
    for k in range(2):
        total = y_recv[0, k]
        for i in range(1, 8):
            total = total + y_recv[i, k]
        y_out[k] = total

    for copy in r_copies:
        copy.wait()
    total = d_ring[0]
    for i in range(1, RING):
        total = total + d_ring[i]
    d_out[core, place] = total
    g_copies = []
    for step in range(1, 8):
        copy = remote(d_out.at[core, place], d_out.at[core, place], g_ssem.at[step], g_rsem.at[step], chip(step))
        copy.start()
        g_copies.append(copy)
    for copy in g_copies:
        copy.wait()
    last = remote(d_out.at[core], d_out.at[core], c_ssem.at[2], c_rsem.at[2], sibling)
    last.start()
    last.wait()

    def sent(s, carry):
        for way in range(2):
            _, to_z, to_x = roles(way, s)

            @pl.when(to_z)
            def _():
                z_copy(way, s).wait_send()

            @pl.when(to_x)
            def _():
                x_copy(way, s).wait_send()

        return carry

    lax.fori_loop(0, STEPS, sent, 0)


def local(ancestor_inverse, factor_panel, structure, block_map, diag_inverse):
    row_count = lax.axis_size("prow")
    p = lax.axis_index("prow")
    q = lax.axis_index("pcol")
    blocks = block_map.shape[0]
    ids = jnp.arange(blocks, dtype=jnp.int32)
    in_structure = jnp.any(structure[:, :, None] == ids[None, None, :], axis=1)
    live = jnp.any(in_structure[:, :, None] & (block_map[None, :, None] == ids[None, None, :]), axis=1)
    live = live.astype(F32).reshape(2, 10, row_count)
    live_own = lax.dynamic_index_in_dim(live, p, 2, keepdims=False)
    live_col = lax.dynamic_index_in_dim(live, q, 2, keepdims=False)
    share_live = lax.dynamic_slice_in_dim(jnp.repeat(live_own, 128, axis=1), q * 80, 80, 1)

    dma = pltpu.SemaphoreType.DMA
    vmem = pltpu.VMEM
    columns, terms = pl.pallas_call(
        kernel,
        name="panel_product",
        out_shape=(jax.ShapeDtypeStruct((2, 80, 256), F32), jax.ShapeDtypeStruct((2, 8, 32, 256), F32)),
        in_specs=[pl.BlockSpec(memory_space=pltpu.SMEM)] * 2 + [pl.BlockSpec(memory_space=pl.ANY)] * 2,
        out_specs=(pl.BlockSpec(memory_space=pltpu.VMEM),) * 2,
        scratch_shapes=[
            vmem((12800, 128), F32), vmem((1280, 1280), BF16), vmem((1280, 1280), BF16),
            vmem((2, 10, 128, 256), F32), vmem((256, 1280), BF16), vmem((256, 1280), BF16),
            vmem((2, 10, 128, 256), F32), vmem((1280, 256), BF16), vmem((1280, 256), BF16),
            vmem((2, 8, 2, 80, 256), F32), vmem((2, 8, 80, 256), F32), vmem((8, 2, 80, 256), F32),
            vmem((8, 2, 80, 256), F32),
            vmem((2, 8, 32, 256), F32), vmem((8, 32, 256), F32), vmem((8, 32, 256), F32), vmem((8, 32, 256), F32),
            vmem((2, 32, 256), F32), vmem((RING, 32, 256), F32),
            dma((3,)), dma((2, STEPS)), dma((2, STEPS)), dma((2, STEPS)), dma((2, STEPS)), dma((3,)), dma((3,)),
            dma((8,)), dma((8,)), dma((8,)), dma((8,)), dma, dma, dma((RING,)), dma((RING,)), dma((8,)), dma((8,)),
        ],
        compiler_params=pltpu.CompilerParams(collective_id=0, has_side_effects=True, vmem_limit_bytes=50 * 2**20),
    )(live_own, live_col, ancestor_inverse.reshape(12800, 128), factor_panel.reshape(2, 10, 128, 256))
    columns = -columns * share_live[:, :, None]
    return columns[:, None, None], diag_inverse + terms.reshape(2, 256, 256)


def solution(mesh):
    in_specs = (
        P(None, "prow", None, None, "pcol", None),
        P(None, None, "prow", None, None),
        P(),
        P(),
        P(),
    )
    out_specs = (P(None, "prow", "pcol", None, None), P())
    return jax.shard_map(local, mesh=mesh, in_specs=in_specs, out_specs=out_specs, check_vma=False)
```

```python
import functools

import jax
import jax.numpy as jnp
from jax import lax
from jax.experimental import pallas as pl
from jax.experimental.pallas import tpu as pltpu
from jax.sharding import PartitionSpec as P

MESH = pl.DeviceIdType.MESH
F32 = jnp.float32
BF16 = jnp.bfloat16

RING = 8
SUBS = 2
ROWS = 64 // SUBS
STEPS = 2 * 10 * SUBS
LAG = 8
TAIL = 2
SHARED = True


def split(value):
    high = value.astype(BF16)
    return high, (value - high.astype(F32)).astype(BF16)


def three_dots(a_high, a_low, b_high, b_low):
    dot = functools.partial(jnp.dot, preferred_element_type=F32)
    return dot(a_high, b_high) + (dot(a_high, b_low) + dot(a_low, b_high))


def kernel(
    live_own, live_col, a_hbm, panel_hbm,
    y_out, d_out,
    a_raw, a_high, a_low, own, own_high, own_low, x, x_high, x_low,
    y, y_peer, y_send, y_recv, d_part, d_peer, d_send, d_recv, d_pair, d_ring,
    load_sem, z_ssem, z_rsem, x_ssem, x_rsem, i_ssem, c_ssem, c_rsem, y_ssem, y_rsem, d_ssem, d_rsem, p_ssem, p_rsem,
    r_ssem, r_rsem, g_ssem, g_rsem,
):
    p = lax.axis_index("prow")
    q = lax.axis_index("pcol")
    half = p // RING
    z = p % RING
    place = q // 2
    core = q % 2
    root_half = q // RING
    hops = (z - q % RING + RING) % RING
    on_root = half == root_half

    across = ((1 - half) * RING + z, q)
    sibling = (p, place * 2 + 1 - core)

    def ring(step):
        return (half * RING + (z + step) % RING, q)

    def chip(step):
        return (p, ((place + step) % 8) * 2 + core)

    row_place = p // 2
    turn = (place // 2 - row_place // 2 + 5) % 4
    injects = (turn < 3) & (place % 2 != row_place % 2) & (core == p % 2)
    entry = ((1 - half) * RING + z, p)
    root = (root_half * RING + q % RING, q)

    def source(i):
        return (root[0], (((place // 2 + 3 + i) % 4) * 2 + 1 - place % 2) * 2 + core)

    load_own = pltpu.make_async_copy(panel_hbm, own, load_sem.at[0])
    load_own.start()
    load_root = pltpu.make_async_copy(panel_hbm, x, load_sem.at[1])

    @pl.when(p == q)
    def _():
        load_root.start()

    load_a = pltpu.make_async_copy(a_hbm, a_raw, load_sem.at[2])
    load_a.start()

    barrier = pltpu.get_barrier_semaphore()
    partners = [across, sibling] + [ring(i) for i in range(1, RING)] + [chip(i) for i in range(1, 8)]
    for partner in partners:
        pl.semaphore_signal(barrier, inc=1, device_id=partner, device_id_type=MESH)
    entered = (hops == 0) & jnp.logical_not(on_root)

    @pl.when(entered)
    def _():
        for i in range(3):
            pl.semaphore_signal(barrier, inc=1, device_id=source(i), device_id_type=MESH)

    @pl.when(injects)
    def _():
        pl.semaphore_signal(barrier, inc=1, device_id=entry, device_id_type=MESH)

    extra = jnp.where(entered, 3, 0) + jnp.where(injects, 1, 0)
    pl.semaphore_wait(barrier, len(partners) + extra)

    @pl.when(p == q)
    def _():
        load_root.wait()

    def chunk(way, s):
        block = s // SUBS
        row = way * 64 + (s % SUBS) * ROWS
        return x.at[block // 10, block % 10, pl.ds(row, ROWS)]

    def z_copy(way, s):
        return pltpu.make_async_remote_copy(
            src_ref=chunk(way, s), dst_ref=chunk(way, s), send_sem=z_ssem.at[way, s], recv_sem=z_rsem.at[way, s],
            device_id=ring(1 if way == 0 else RING - 1), device_id_type=MESH,
        )

    def x_copy(way, s):
        return pltpu.make_async_remote_copy(
            src_ref=chunk(way, s), dst_ref=chunk(way, s), send_sem=x_ssem.at[way, s], recv_sem=x_rsem.at[way, s],
            device_id=across, device_id_type=MESH,
        )

    def roles(way, s):
        if SHARED:
            kind = s % 3
            both = kind == 2
            carries = both | (on_root & (kind == 0)) | (jnp.logical_not(on_root) & (kind == 1))
        else:
            both = jnp.bool_(True)
            carries = jnp.bool_(True)
        done = hops if way == 0 else (RING - hops) % RING
        to_z = carries & (done < RING - 1)
        to_x = (hops != 0) & carries & jnp.logical_not(both)
        return carries, to_z, to_x

    def event(way, s):
        carries, to_z, to_x = roles(way, s)

        @pl.when((hops == 0) & jnp.logical_not(on_root))
        def _():
            x_copy(way, s).wait_recv()

        @pl.when((hops != 0) & carries)
        def _():
            z_copy(way, s).wait_recv()

        @pl.when(to_z)
        def _():
            z_copy(way, s).start()

        @pl.when(to_x)
        def _():
            x_copy(way, s).start()

    def i_copy(way, s):
        block = s // SUBS
        row = way * 64 + (s % SUBS) * ROWS
        src = own.at[block // 10, block % 10, pl.ds(row, ROWS)]
        return pltpu.make_async_remote_copy(
            src_ref=src, dst_ref=chunk(way, s), send_sem=i_ssem.at[way, s], recv_sem=x_rsem.at[way, s],
            device_id=entry, device_id_type=MESH,
        )

    def inject(s, carry):
        for way in range(2):

            @pl.when((2 * s + way) % 3 == turn)
            def _():
                i_copy(way, s).start()

        return carry

    load_own.wait()

    @pl.when(injects)
    def _():
        lax.fori_loop(0, STEPS, inject, 0)

    shift = jnp.where(hops == 0, 0, (RING - 2 * hops) * LAG)
    late_up = jnp.maximum(0, -shift)
    late_down = jnp.maximum(0, shift)

    def remote(src, dst, send, recv, device):
        return pltpu.make_async_remote_copy(
            src_ref=src, dst_ref=dst, send_sem=send, recv_sem=recv, device_id=device, device_id_type=MESH
        )

    def split_a(i):
        for col in range(10):
            high, low = split(a_raw[pl.ds(i * 640 + col, 64, stride=10), :])
            rows = pl.ds(pl.multiple_of(i * 64, 64), 64)
            a_high[rows, col * 128 : (col + 1) * 128] = high
            a_low[rows, col * 128 : (col + 1) * 128] = low

    def split_own(i):
        k, r = i // 10, i % 10
        rows = pl.ds(pl.multiple_of(r * 128, 128), 128)
        high, low = split((own[k, r] * live_own[k, r]).T)
        own_high[k, :, rows] = high
        own_low[k, :, rows] = low

    def arrived(s):
        for way in range(2):
            carries, _, _ = roles(way, s)

            @pl.when((hops != 0) & jnp.logical_not(carries))
            def _():
                x_copy(way, s).wait_recv()

    def take_block(k, r):
        if SHARED:
            for sub in range(SUBS):
                arrived((k * 10 + r) * SUBS + sub)
        rows = pl.ds(pl.multiple_of(r * 128, 128), 128)
        high, low = split(x[k, r] * live_col[k, r])
        x_high[rows] = high
        x_low[rows] = low

    def rows_of_y(k, m):
        rows = pl.ds(pl.multiple_of(m * 160, 32), 160)
        part = three_dots(a_high[rows], a_low[rows], x_high[...], x_low[...])
        y[k, m] = part.reshape(2, 80, 256)

    def terms(k):
        y_high, y_low = split(y[k].reshape(1280, 256))
        d_part[k] = three_dots(own_high[k], own_low[k], y_high, y_low).reshape(2, 8, 16, 256)

    def peer_d(k):
        return remote(d_part.at[k, 1 - core], d_peer.at[k], c_ssem.at[k, 0], c_rsem.at[k, 0], sibling)

    def peer_y(k):
        return remote(y.at[k, :, 1 - core], y_peer.at[k], c_ssem.at[k, 1], c_rsem.at[k, 1], sibling)

    def chip_d(k, step):
        to = (place + step) % 8
        return remote(d_send.at[k, to], d_recv.at[k, place], d_ssem.at[k, step], d_rsem.at[k, step], chip(step))

    def chip_y(k, step):
        to = (place + step) % 8
        return remote(y_send.at[k, to], y_recv.at[k, place], y_ssem.at[k, step], y_rsem.at[k, step], chip(step))

    def pair(k):
        return remote(d_pair.at[k, 0], d_pair.at[k, 1], p_ssem.at[k], p_rsem.at[k], across)

    def round_z(k, step):
        return remote(d_ring.at[k, z], d_ring.at[k, z], r_ssem.at[k, step], r_rsem.at[k, step], ring(step))

    def gather(k, step):
        mine = d_out.at[k, core, place]
        return remote(mine, mine, g_ssem.at[k, step], g_rsem.at[k, step], chip(step))

    def peer_out(k):
        mine = d_out.at[k, core]
        return remote(mine, mine, c_ssem.at[k, 2], c_rsem.at[k, 2], sibling)

    def to_sibling(k):
        peer_d(k).start()
        peer_y(k).start()

    def to_chips(k):
        peer_d(k).wait()
        for i in range(8):
            d_send[k, i] = d_part[k, core, i] + d_peer[k, i]
        for step in range(1, 8):
            chip_d(k, step).start()
        d_recv[k, place] = d_send[k, place]
        peer_y(k).wait()
        for i in range(8):
            y_send[k, i] = y[k, i, core] + y_peer[k, i]
        for step in range(1, 8):
            chip_y(k, step).start()
        y_recv[k, place] = y_send[k, place]

    def to_across(k):
        for step in range(1, 8):
            chip_d(k, step).wait()
        total = d_recv[k, 0]
        for i in range(1, 8):
            total = total + d_recv[k, i]
        d_pair[k, 0] = total
        pair(k).start()

    def to_ring(k):
        pair(k).wait()
        d_ring[k, z] = d_pair[k, 0] + d_pair[k, 1]
        for step in range(1, RING):
            round_z(k, step).start()

    def to_gather(k):
        for step in range(1, RING):
            round_z(k, step).wait()
        total = d_ring[k, 0]
        for i in range(1, RING):
            total = total + d_ring[k, i]
        d_out[k, core, place] = total
        for step in range(1, 8):
            gather(k, step).start()

    def to_out(k):
        for step in range(1, 8):
            gather(k, step).wait()
        peer_out(k).start()

    def sum_y(k):
        for step in range(1, 8):
            chip_y(k, step).wait()
        total = y_recv[k, 0]
        for i in range(1, 8):
            total = total + y_recv[k, i]
        y_out[k] = total

    load_a.wait()
    begin = jnp.where(hops == 0, STEPS, STEPS // 2 + jnp.maximum(late_up, late_down))

    def stream(t, carry):
        for way, late in ((0, late_up), (1, late_down)):
            s = t - late

            @pl.when((s >= 0) & (s < STEPS))
            def _():
                event(way, s)

        @pl.when(t < 20)
        def _():
            split_a(t)
            split_own(t)

        work = t - begin

        @pl.when((work >= 0) & (work < 5))
        def _():
            for i in range(2):
                take_block(0, work * 2 + i)

        @pl.when((work >= 5) & (work < 13))
        def _():
            rows_of_y(0, work - 5)

        @pl.when(work == 13)
        def _():
            terms(0)
            to_sibling(0)

        @pl.when(work == 20)
        def _():
            to_chips(0)

        return carry

    lax.fori_loop(0, STEPS + 6 * LAG + TAIL, stream, 0)

    def take(r, carry):
        take_block(1, r)
        return carry

    lax.fori_loop(0, 10, take, 0)
    to_across(0)

    def rows_of(m, carry):
        rows_of_y(1, m)
        return carry

    lax.fori_loop(0, 4, rows_of, 0)
    to_ring(0)
    lax.fori_loop(4, 8, rows_of, 0)
    terms(1)
    to_sibling(1)
    to_gather(0)
    to_chips(1)
    sum_y(0)
    to_across(1)
    to_out(0)
    to_ring(1)
    sum_y(1)
    to_gather(1)
    to_out(1)
    for k in range(2):
        peer_out(k).wait()

    def sent(s, carry):
        for way in range(2):
            _, to_z, to_x = roles(way, s)

            @pl.when(to_z)
            def _():
                z_copy(way, s).wait_send()

            @pl.when(to_x)
            def _():
                x_copy(way, s).wait_send()

            @pl.when(injects & ((2 * s + way) % 3 == turn))
            def _():
                i_copy(way, s).wait_send()

        return carry

    lax.fori_loop(0, STEPS, sent, 0)


def local(ancestor_inverse, factor_panel, structure, block_map, diag_inverse):
    row_count = lax.axis_size("prow")
    p = lax.axis_index("prow")
    q = lax.axis_index("pcol")
    blocks = block_map.shape[0]
    ids = jnp.arange(blocks, dtype=jnp.int32)
    in_structure = jnp.any(structure[:, :, None] == ids[None, None, :], axis=1)
    live = jnp.any(in_structure[:, :, None] & (block_map[None, :, None] == ids[None, None, :]), axis=1)
    live = live.astype(F32).reshape(2, 10, row_count)
    live_own = lax.dynamic_index_in_dim(live, p, 2, keepdims=False)
    live_col = lax.dynamic_index_in_dim(live, q, 2, keepdims=False)
    share_live = lax.dynamic_slice_in_dim(jnp.repeat(live_own, 128, axis=1), q * 80, 80, 1)

    dma = pltpu.SemaphoreType.DMA
    vmem = pltpu.VMEM
    columns, terms = pl.pallas_call(
        kernel,
        name="panel_product",
        out_shape=(jax.ShapeDtypeStruct((2, 80, 256), F32), jax.ShapeDtypeStruct((2, 2, 8, 16, 256), F32)),
        in_specs=[pl.BlockSpec(memory_space=pltpu.SMEM)] * 2 + [pl.BlockSpec(memory_space=pl.ANY)] * 2,
        out_specs=(pl.BlockSpec(memory_space=pltpu.VMEM),) * 2,
        scratch_shapes=[
            vmem((12800, 128), F32), vmem((1280, 1280), BF16), vmem((1280, 1280), BF16),
            vmem((2, 10, 128, 256), F32), vmem((2, 256, 1280), BF16), vmem((2, 256, 1280), BF16),
            vmem((2, 10, 128, 256), F32), vmem((1280, 256), BF16), vmem((1280, 256), BF16),
            vmem((2, 8, 2, 80, 256), F32), vmem((2, 8, 80, 256), F32), vmem((2, 8, 80, 256), F32),
            vmem((2, 8, 80, 256), F32),
            vmem((2, 2, 8, 16, 256), F32), vmem((2, 8, 16, 256), F32), vmem((2, 8, 16, 256), F32),
            vmem((2, 8, 16, 256), F32), vmem((2, 2, 16, 256), F32), vmem((2, RING, 16, 256), F32),
            dma((3,)), dma((2, STEPS)), dma((2, STEPS)), dma((2, STEPS)), dma((2, STEPS)), dma((2, STEPS)),
            dma((2, 3)), dma((2, 3)), dma((2, 8)), dma((2, 8)), dma((2, 8)), dma((2, 8)), dma((2,)), dma((2,)),
            dma((2, RING)), dma((2, RING)), dma((2, 8)), dma((2, 8)),
        ],
        compiler_params=pltpu.CompilerParams(collective_id=0, has_side_effects=True, vmem_limit_bytes=50 * 2**20),
    )(live_own, live_col, ancestor_inverse.reshape(12800, 128), factor_panel.reshape(2, 10, 128, 256))
    columns = -columns * share_live[:, :, None]
    return columns[:, None, None], diag_inverse + terms.reshape(2, 256, 256)


def solution(mesh):
    in_specs = (
        P(None, "prow", None, None, "pcol", None),
        P(None, None, "prow", None, None),
        P(),
        P(),
        P(),
    )
    out_specs = (P(None, "prow", "pcol", None, None), P())
    return jax.shard_map(local, mesh=mesh, in_specs=in_specs, out_specs=out_specs, check_vma=False)
```

```python
import functools

import jax
import jax.numpy as jnp
from jax import lax
from jax.experimental import pallas as pl
from jax.experimental.pallas import tpu as pltpu
from jax.sharding import PartitionSpec as P

MESH = pl.DeviceIdType.MESH
F32 = jnp.float32
BF16 = jnp.bfloat16

RING = 8
SUBS = 2
ROWS = 64 // SUBS
STEPS = 2 * 10 * SUBS
PERIOD = 2
APART = 12
LEAD = 8
SLACK = 4
HALF = STEPS // 2


def split(value):
    high = value.astype(BF16)
    return high, (value - high.astype(F32)).astype(BF16)


def three_dots(a_high, a_low, b_high, b_low):
    dot = functools.partial(jnp.dot, preferred_element_type=F32)
    return dot(a_high, b_high) + (dot(a_high, b_low) + dot(a_low, b_high))


def kernel(
    live_own, live_col, a_hbm, panel_hbm,
    y_out, d_out,
    a_raw, a_high, a_low, own, own_high, own_low, u_high, u_low, x, x_high, x_low,
    y, y_peer, y_send, y_recv, d_part, d_peer, d_send, d_recv, d_ring,
    load_sem, z_ssem, z_rsem, x_ssem, x_rsem, i_ssem, c_ssem, c_rsem, y_ssem, y_rsem, d_ssem, d_rsem,
    r_ssem, r_rsem, g_ssem, g_rsem, m_ssem, m_rsem,
):
    p = lax.axis_index("prow")
    q = lax.axis_index("pcol")
    half = p // RING
    z = p % RING
    place = q // 2
    core = q % 2
    root_half = q // RING
    hops = (z - q % RING + RING) % RING
    on_root = half == root_half

    spot = half * 8 + place
    across = ((1 - half) * RING + z, q)
    sibling = (p, place * 2 + 1 - core)

    def ring(step):
        return (half * RING + (z + step) % RING, q)

    def chip(step):
        return (p, ((place + step) % 8) * 2 + core)

    def plane(step):
        to = (spot + step) % 16
        return ((to // 8) * RING + z, (to % 8) * 2 + core)

    row_place = p // 2
    turn = (place // 2 - row_place // 2 + 4) % 4
    injects = (place % 2 != row_place % 2) & (core == p % 2)
    entry = ((1 - half) * RING + z, p)
    root = (root_half * RING + q % RING, q)

    def source(i):
        return (root[0], (((place // 2 + i) % 4) * 2 + 1 - place % 2) * 2 + core)

    load_own = pltpu.make_async_copy(panel_hbm, own, load_sem.at[0])
    load_own.start()
    load_root = pltpu.make_async_copy(panel_hbm, x, load_sem.at[1])

    @pl.when(p == q)
    def _():
        load_root.start()

    load_a = pltpu.make_async_copy(a_hbm, a_raw, load_sem.at[2])
    load_a.start()

    barrier = pltpu.get_barrier_semaphore()
    partners = [sibling] + [ring(i) for i in range(1, RING)] + [plane(i) for i in range(1, 16)]
    for partner in partners:
        pl.semaphore_signal(barrier, inc=1, device_id=partner, device_id_type=MESH)
    entered = (hops == 0) & jnp.logical_not(on_root)

    @pl.when(entered)
    def _():
        for i in range(4):
            pl.semaphore_signal(barrier, inc=1, device_id=source(i), device_id_type=MESH)

    @pl.when(injects)
    def _():
        pl.semaphore_signal(barrier, inc=1, device_id=entry, device_id_type=MESH)

    extra = jnp.where(entered, 4, 0) + jnp.where(injects, 1, 0)
    pl.semaphore_wait(barrier, len(partners) + extra)

    @pl.when(p == q)
    def _():
        load_root.wait()

    def rows_of_chunk(way, s):
        row = lax.div(s, SUBS) * 128 + way * 64 + lax.rem(s, SUBS) * ROWS
        return pl.ds(pl.multiple_of(row, ROWS), ROWS)

    def chunk(way, s):
        return x.at[rows_of_chunk(way, s)]

    def z_copy(way, s, step):
        return pltpu.make_async_remote_copy(
            src_ref=chunk(way, s), dst_ref=chunk(way, s), send_sem=z_ssem.at[min(step - 1, 1), way, s],
            recv_sem=z_rsem.at[way, s], device_id=ring(step), device_id_type=MESH,
        )

    def x_copy(way, s):
        return pltpu.make_async_remote_copy(
            src_ref=chunk(way, s), dst_ref=chunk(way, s), send_sem=x_ssem.at[way, s], recv_sem=x_rsem.at[way, s],
            device_id=across, device_id_type=MESH,
        )

    def roles(way, s):
        kind = lax.rem(s, PERIOD)
        both = kind >= 2
        carries = both | (kind == jnp.where(on_root, 0, 1))
        up = carries & (hops < RING // 2)
        down = carries & ((hops == 0) | (hops > RING // 2 + 1))
        to_x = (hops != 0) & carries & jnp.logical_not(both)
        return carries, up, down, to_x

    def event(way, s):
        carries, up, down, to_x = roles(way, s)

        @pl.when((hops == 0) & jnp.logical_not(on_root))
        def _():
            x_copy(way, s).wait_recv()

        @pl.when((hops != 0) & carries)
        def _():
            z_copy(way, s, 1).wait_recv()

        @pl.when(up)
        def _():
            z_copy(way, s, 1).start()

        @pl.when(down)
        def _():
            z_copy(way, s, RING - 1).start()

        @pl.when(to_x)
        def _():
            x_copy(way, s).start()

    def i_copy(way, s):
        src = own.at[rows_of_chunk(way, s)]
        return pltpu.make_async_remote_copy(
            src_ref=src, dst_ref=chunk(way, s), send_sem=i_ssem.at[way, s], recv_sem=x_rsem.at[way, s],
            device_id=entry, device_id_type=MESH,
        )

    def entry_copy(j):
        way = lax.rem(turn, 2)
        return i_copy(way, 2 * j + lax.div(turn, 2))

    def inject(j, carry):
        entry_copy(j).start()
        return carry

    load_own.wait()

    @pl.when(injects)
    def _():
        lax.fori_loop(0, LEAD, inject, 0)

    def remote(src, dst, send, recv, device):
        return pltpu.make_async_remote_copy(
            src_ref=src, dst_ref=dst, send_sem=send, recv_sem=recv, device_id=device, device_id_type=MESH
        )

    def split_a(i):
        for col in range(10):
            high, low = split(a_raw[pl.ds(i * 640 + col, 64, stride=10), :])
            rows = pl.ds(pl.multiple_of(i * 64, 64), 64)
            a_high[rows, col * 128 : (col + 1) * 128] = high
            a_low[rows, col * 128 : (col + 1) * 128] = low

    def split_own(i):
        k, r = lax.div(i, 10), lax.rem(i, 10)
        rows = pl.ds(pl.multiple_of(r * 128, 128), 128)
        high, low = split((own[pl.ds(pl.multiple_of(i * 128, 128), 128)] * live_own[k, r]).T)
        own_high[k, :, rows] = high
        own_low[k, :, rows] = low

    def arrived(s):
        for way in range(2):
            carries, _, _, _ = roles(way, s)

            @pl.when((hops != 0) & jnp.logical_not(carries))
            def _():
                x_copy(way, s).wait_recv()

    def take_block(k, r):
        for sub in range(SUBS):
            arrived((k * 10 + r) * SUBS + sub)
        rows = pl.ds(pl.multiple_of(r * 128, 128), 128)
        high, low = split(x[pl.ds(pl.multiple_of((k * 10 + r) * 128, 128), 128)] * live_col[k, r])
        x_high[k, rows] = high
        x_low[k, rows] = low

    def rows_of_y(k, m):
        rows = pl.ds(pl.multiple_of(m * 160, 32), 160)
        part = three_dots(a_high[rows], a_low[rows], x_high[k], x_low[k])
        y[k, m] = part.reshape(2, 80, 256)

    def left_product(i):
        k = lax.div(i, 5)
        cols = pl.ds(pl.multiple_of(lax.rem(i, 5) * 256, 256), 256)
        high, low = split(three_dots(own_high[k], own_low[k], a_high[:, cols], a_low[:, cols]))
        u_high[k, :, cols] = high
        u_low[k, :, cols] = low

    def terms(k):
        d_part[k] = three_dots(u_high[k], u_low[k], x_high[k], x_low[k]).reshape(2, 16, 8, 256)
        peer_d(k).start()

    def peer_d(k):
        return remote(d_part.at[k, 1 - core], d_peer.at[k], c_ssem.at[k, 0], c_rsem.at[k, 0], sibling)

    def peer_rows(k, i):
        m = lax.rem(place + 1 + i, 8)
        return remote(y.at[k, m, 1 - core], y_peer.at[k, m], m_ssem.at[k, i], m_rsem.at[k, i], sibling)

    def rows_to_peer(k, i):
        rows_of_y(k, lax.rem(place + 1 + i, 8))
        peer_rows(k, i).start()

    def rows_to_chip(k, i):
        m = lax.rem(place + 1 + i, 8)
        peer_rows(k, i).wait()
        y_send[k, m] = y[k, m, core] + y_peer[k, m]

        @pl.when(i < 7)
        def _():
            chip_y(k, i + 1).start()

        @pl.when(i == 7)
        def _():
            y_recv[k, place] = y_send[k, place]

    def plane_d(k, step):
        to = (spot + step) % 16
        return remote(d_send.at[k, to], d_recv.at[k, spot], d_ssem.at[k, step], d_rsem.at[k, step], plane(step))

    def chip_y(k, step):
        to = (place + step) % 8
        return remote(y_send.at[k, to], y_recv.at[k, place], y_ssem.at[k, step], y_rsem.at[k, step], chip(step))

    def round_z(step):
        return remote(d_ring.at[z], d_ring.at[z], r_ssem.at[step], r_rsem.at[step], ring(step))

    def gather(step):
        mine = d_out.at[:, core, spot]
        return remote(mine, mine, g_ssem.at[step], g_rsem.at[step], plane(step))

    def peer_out():
        mine = d_out.at[:, core]
        return remote(mine, mine, c_ssem.at[0, 2], c_rsem.at[0, 2], sibling)

    def d_to_plane(k):
        peer_d(k).wait()
        d_send[k] = d_part[k, core] + d_peer[k]
        for step in range(1, 16):
            plane_d(k, step).start()
        d_recv[k, spot] = d_send[k, spot]

    def d_to_ring():
        for k in range(2):
            for step in range(1, 16):
                plane_d(k, step).wait()
            total = d_recv[k, 0]
            for i in range(1, 16):
                total = total + d_recv[k, i]
            d_ring[z, k] = total
        for step in range(1, RING):
            round_z(step).start()

    def d_to_gather():
        for step in range(1, RING):
            round_z(step).wait()
        for k in range(2):
            total = d_ring[0, k]
            for i in range(1, RING):
                total = total + d_ring[i, k]
            d_out[k, core, spot] = total
        for step in range(1, 16):
            gather(step).start()

    def sum_y(k):
        for step in range(1, 8):
            chip_y(k, step).wait()
        total = y_recv[k, 0]
        for i in range(1, 8):
            total = total + y_recv[k, i]
        y_out[k] = total

    load_a.wait()
    begin = jnp.where(hops == 0, STEPS, max(HALF, 26))
    begin_last = HALF + SUBS + SLACK

    def stream(t, carry):
        @pl.when(t < STEPS)
        def _():
            event(0, t)
            event(1, t)

        @pl.when(injects & (t < STEPS // 2 - LEAD))
        def _():
            entry_copy(t + LEAD).start()

        @pl.when(t < 20)
        def _():
            split_a(t)
            split_own(t)

        work = t - begin

        @pl.when((work >= 0) & (work < 5))
        def _():
            for i in range(2):
                take_block(0, work * 2 + i)

        @pl.when(work == 5)
        def _():
            terms(0)

        @pl.when((work >= 6) & (work < 14))
        def _():
            rows_to_peer(0, work - 6)

        @pl.when((work >= 6 + APART) & (work < 14 + APART))
        def _():
            rows_to_chip(0, work - 6 - APART)

        @pl.when(work == 5 + APART)
        def _():
            d_to_plane(0)

        @pl.when((t >= 20) & (t < 30))
        def _():
            left_product(t - 20)

        block = lax.div(t - begin_last, SUBS)

        @pl.when((t >= begin_last) & (block < 10) & (lax.rem(t - begin_last, SUBS) == 0))
        def _():
            take_block(1, block)

        return carry

    lax.fori_loop(0, STEPS + 14 + APART, stream, 0)

    terms(1)

    def last_rows(i, carry):
        @pl.when(i < 8)
        def _():
            rows_to_peer(1, i)

        @pl.when(i == 1)
        def _():
            d_to_plane(1)

        @pl.when(i >= 2)
        def _():
            rows_to_chip(1, i - 2)

        @pl.when(i == 6)
        def _():
            d_to_ring()

        return carry

    lax.fori_loop(0, 10, last_rows, 0)
    sum_y(0)
    def sent(s, carry):
        for way in range(2):
            _, up, down, to_x = roles(way, s)

            @pl.when(up)
            def _():
                z_copy(way, s, 1).wait_send()

            @pl.when(down)
            def _():
                z_copy(way, s, RING - 1).wait_send()

            @pl.when(to_x)
            def _():
                x_copy(way, s).wait_send()

        return carry

    lax.fori_loop(0, STEPS, sent, 0)

    def entered_all(j, carry):
        entry_copy(j).wait_send()
        return carry

    @pl.when(injects)
    def _():
        lax.fori_loop(0, STEPS // 2, entered_all, 0)

    d_to_gather()
    sum_y(1)
    for step in range(1, 16):
        gather(step).wait()
    peer_out().start()
    peer_out().wait()


def local(ancestor_inverse, factor_panel, structure, block_map, diag_inverse):
    row_count = lax.axis_size("prow")
    p = lax.axis_index("prow")
    q = lax.axis_index("pcol")
    blocks = block_map.shape[0]
    ids = jnp.arange(blocks, dtype=jnp.int32)
    in_structure = jnp.any(structure[:, :, None] == ids[None, None, :], axis=1)
    live = jnp.any(in_structure[:, :, None] & (block_map[None, :, None] == ids[None, None, :]), axis=1)
    live = live.astype(F32).reshape(2, 10, row_count)
    live_own = lax.dynamic_index_in_dim(live, p, 2, keepdims=False)
    live_col = lax.dynamic_index_in_dim(live, q, 2, keepdims=False)
    share_live = lax.dynamic_slice_in_dim(jnp.repeat(live_own, 128, axis=1), q * 80, 80, 1)

    dma = pltpu.SemaphoreType.DMA
    vmem = pltpu.VMEM
    columns, terms = pl.pallas_call(
        kernel,
        name="panel_product",
        out_shape=(jax.ShapeDtypeStruct((2, 80, 256), F32), jax.ShapeDtypeStruct((2, 2, 16, 8, 256), F32)),
        in_specs=[pl.BlockSpec(memory_space=pltpu.SMEM)] * 2 + [pl.BlockSpec(memory_space=pl.ANY)] * 2,
        out_specs=(pl.BlockSpec(memory_space=pltpu.VMEM),) * 2,
        scratch_shapes=[
            vmem((12800, 128), F32), vmem((1280, 1280), BF16), vmem((1280, 1280), BF16),
            vmem((2560, 256), F32), vmem((2, 256, 1280), BF16), vmem((2, 256, 1280), BF16),
            vmem((2, 256, 1280), BF16), vmem((2, 256, 1280), BF16),
            vmem((2560, 256), F32), vmem((2, 1280, 256), BF16), vmem((2, 1280, 256), BF16),
            vmem((2, 8, 2, 80, 256), F32), vmem((2, 8, 80, 256), F32), vmem((2, 8, 80, 256), F32),
            vmem((2, 8, 80, 256), F32),
            vmem((2, 2, 16, 8, 256), F32), vmem((2, 16, 8, 256), F32), vmem((2, 16, 8, 256), F32),
            vmem((2, 16, 8, 256), F32), vmem((RING, 2, 8, 256), F32),
            dma((3,)), dma((2, 2, STEPS)), dma((2, STEPS)), dma((2, STEPS)), dma((2, STEPS)), dma((2, STEPS)),
            dma((2, 3)), dma((2, 3)), dma((2, 8)), dma((2, 8)), dma((2, 16)), dma((2, 16)),
            dma((RING,)), dma((RING,)), dma((16,)), dma((16,)), dma((2, 8)), dma((2, 8)),
        ],
        compiler_params=pltpu.CompilerParams(collective_id=0, has_side_effects=True, vmem_limit_bytes=50 * 2**20),
    )(live_own, live_col, ancestor_inverse.reshape(12800, 128), factor_panel.reshape(2560, 256))
    columns = -columns * share_live[:, :, None]
    return columns[:, None, None], diag_inverse + terms.reshape(2, 256, 256)


def solution(mesh):
    in_specs = (
        P(None, "prow", None, None, "pcol", None),
        P(None, None, "prow", None, None),
        P(),
        P(),
        P(),
    )
    out_specs = (P(None, "prow", "pcol", None, None), P())
    return jax.shard_map(local, mesh=mesh, in_specs=in_specs, out_specs=out_specs, check_vma=False)
```

```python
import functools

import jax
import jax.numpy as jnp
from jax import lax
from jax.experimental import pallas as pl
from jax.experimental.pallas import tpu as pltpu
from jax.sharding import PartitionSpec as P

MESH = pl.DeviceIdType.MESH
F32 = jnp.float32
BF16 = jnp.bfloat16

RING = 8
SUBS = 2
ROWS = 64 // SUBS
STEPS = 2 * 10 * SUBS
PERIOD = 2
APART = 12
LEAD = 8
SLACK = 4
HALF = STEPS // 2


def split(value):
    high = value.astype(BF16)
    return high, (value - high.astype(F32)).astype(BF16)


def three_dots(a_high, a_low, b_high, b_low):
    dot = functools.partial(jnp.dot, preferred_element_type=F32)
    return dot(a_high, b_high) + (dot(a_high, b_low) + dot(a_low, b_high))


def kernel(
    structure, block_map, a_hbm, panel_hbm,
    y_out, d_out,
    live_own, live_col, a_raw, a_high, a_low, own, own_high, own_low, u_high, u_low, x, x_high, x_low,
    y, y_peer, y_send, y_recv, d_part, d_peer, d_send, d_recv, d_ring,
    load_sem, z_ssem, z_rsem, x_ssem, x_rsem, i_ssem, c_ssem, c_rsem, y_ssem, y_rsem, d_ssem, d_rsem,
    r_ssem, r_rsem, g_ssem, g_rsem, m_ssem, m_rsem,
):
    p = lax.axis_index("prow")
    q = lax.axis_index("pcol")
    half = p // RING
    z = p % RING
    place = q // 2
    core = q % 2
    root_half = q // RING
    hops = (z - q % RING + RING) % RING
    on_root = half == root_half

    spot = half * 8 + place
    across = ((1 - half) * RING + z, q)
    sibling = (p, place * 2 + 1 - core)

    def ring(step):
        return (half * RING + (z + step) % RING, q)

    def chip(step):
        return (p, ((place + step) % 8) * 2 + core)

    def plane(step):
        to = (spot + step) % 16
        return ((to // 8) * RING + z, (to % 8) * 2 + core)

    row_place = p // 2
    turn = (place // 2 - row_place // 2 + 4) % 4
    injects = (place % 2 != row_place % 2) & (core == p % 2)
    entry = ((1 - half) * RING + z, p)
    root = (root_half * RING + q % RING, q)

    def source(i):
        return (root[0], (((place // 2 + i) % 4) * 2 + 1 - place % 2) * 2 + core)

    load_own = pltpu.make_async_copy(panel_hbm, own, load_sem.at[0])
    load_own.start()
    load_root = pltpu.make_async_copy(panel_hbm, x, load_sem.at[1])

    @pl.when(p == q)
    def _():
        load_root.start()

    load_a = pltpu.make_async_copy(a_hbm, a_raw, load_sem.at[2])
    load_a.start()

    barrier = pltpu.get_barrier_semaphore()
    partners = [sibling] + [ring(i) for i in range(1, RING)] + [plane(i) for i in range(1, 16)]
    for partner in partners:
        pl.semaphore_signal(barrier, inc=1, device_id=partner, device_id_type=MESH)
    entered = (hops == 0) & jnp.logical_not(on_root)

    @pl.when(entered)
    def _():
        for i in range(4):
            pl.semaphore_signal(barrier, inc=1, device_id=source(i), device_id_type=MESH)

    @pl.when(injects)
    def _():
        pl.semaphore_signal(barrier, inc=1, device_id=entry, device_id_type=MESH)

    lanes = lax.broadcasted_iota(jnp.int32, (1, 256), 1)

    def mark(b, live):
        return tuple(jnp.where(lanes == block_map[structure[k, b]], 1.0, live[k]) for k in range(2))

    live = lax.fori_loop(0, 120, mark, (jnp.zeros((1, 256), F32),) * 2)
    for k in range(2):
        for r in range(10):
            for ref, index in ((live_own, p), (live_col, q)):
                found = jnp.sum(jnp.where(lanes == r * 16 + index, live[k], 0.0), axis=1, keepdims=True)
                ref[k * 10 + r] = jnp.broadcast_to(found, (8, 256))

    extra = jnp.where(entered, 4, 0) + jnp.where(injects, 1, 0)
    pl.semaphore_wait(barrier, len(partners) + extra)

    @pl.when(p == q)
    def _():
        load_root.wait()

    def rows_of_chunk(way, s):
        row = lax.div(s, SUBS) * 128 + way * 64 + lax.rem(s, SUBS) * ROWS
        return pl.ds(pl.multiple_of(row, ROWS), ROWS)

    def chunk(way, s):
        return x.at[rows_of_chunk(way, s)]

    def z_copy(way, s, step):
        return pltpu.make_async_remote_copy(
            src_ref=chunk(way, s), dst_ref=chunk(way, s), send_sem=z_ssem.at[min(step - 1, 1), way, s],
            recv_sem=z_rsem.at[way, s], device_id=ring(step), device_id_type=MESH,
        )

    def x_copy(way, s):
        return pltpu.make_async_remote_copy(
            src_ref=chunk(way, s), dst_ref=chunk(way, s), send_sem=x_ssem.at[way, s], recv_sem=x_rsem.at[way, s],
            device_id=across, device_id_type=MESH,
        )

    def roles(way, s):
        kind = jnp.where(lax.rem(s, 8) == 7, 2, lax.rem(s, PERIOD))
        both = kind >= 2
        carries = both | (kind == jnp.where(on_root, 0, 1))
        up = carries & (hops < RING // 2)
        down = carries & ((hops == 0) | (hops > RING // 2 + 1))
        to_x = (hops != 0) & carries & jnp.logical_not(both)
        return carries, up, down, to_x

    def event(way, s):
        carries, up, down, to_x = roles(way, s)

        @pl.when((hops == 0) & jnp.logical_not(on_root))
        def _():
            x_copy(way, s).wait_recv()

        @pl.when((hops != 0) & carries)
        def _():
            z_copy(way, s, 1).wait_recv()

        @pl.when(up)
        def _():
            z_copy(way, s, 1).start()

        @pl.when(down)
        def _():
            z_copy(way, s, RING - 1).start()

        @pl.when(to_x)
        def _():
            x_copy(way, s).start()

    def i_copy(way, s):
        src = own.at[rows_of_chunk(way, s)]
        return pltpu.make_async_remote_copy(
            src_ref=src, dst_ref=chunk(way, s), send_sem=i_ssem.at[way, s], recv_sem=x_rsem.at[way, s],
            device_id=entry, device_id_type=MESH,
        )

    def entry_copy(j):
        way = lax.rem(turn, 2)
        return i_copy(way, 2 * j + lax.div(turn, 2))

    def inject(j, carry):
        entry_copy(j).start()
        return carry

    load_own.wait()

    @pl.when(injects)
    def _():
        lax.fori_loop(0, LEAD, inject, 0)

    def remote(src, dst, send, recv, device):
        return pltpu.make_async_remote_copy(
            src_ref=src, dst_ref=dst, send_sem=send, recv_sem=recv, device_id=device, device_id_type=MESH
        )

    def split_a(i):
        for col in range(10):
            high, low = split(a_raw[pl.ds(i * 640 + col, 64, stride=10), :])
            rows = pl.ds(pl.multiple_of(i * 64, 64), 64)
            a_high[rows, col * 128 : (col + 1) * 128] = high
            a_low[rows, col * 128 : (col + 1) * 128] = low

    def split_own(i):
        k, r = lax.div(i, 10), lax.rem(i, 10)
        rows = pl.ds(pl.multiple_of(r * 128, 128), 128)
        high, low = split((own[pl.ds(pl.multiple_of(i * 128, 128), 128)] * live_own[i, 0:1]).T)
        own_high[k, :, rows] = high
        own_low[k, :, rows] = low

    def arrived(s):
        for way in range(2):
            carries, _, _, _ = roles(way, s)

            @pl.when((hops != 0) & jnp.logical_not(carries))
            def _():
                x_copy(way, s).wait_recv()

    def take_block(k, r):
        for sub in range(SUBS):
            arrived((k * 10 + r) * SUBS + sub)
        rows = pl.ds(pl.multiple_of(r * 128, 128), 128)
        high, low = split(x[pl.ds(pl.multiple_of((k * 10 + r) * 128, 128), 128)] * live_col[k * 10 + r, 0:1])
        x_high[k, rows] = high
        x_low[k, rows] = low

    def rows_of_y(k, m):
        rows = pl.ds(pl.multiple_of(m * 160, 32), 160)
        part = three_dots(a_high[rows], a_low[rows], x_high[k], x_low[k])
        y[k, m] = part.reshape(2, 80, 256)

    def left_product(i):
        k = lax.div(i, 5)
        cols = pl.ds(pl.multiple_of(lax.rem(i, 5) * 256, 256), 256)
        high, low = split(three_dots(own_high[k], own_low[k], a_high[:, cols], a_low[:, cols]))
        u_high[k, :, cols] = high
        u_low[k, :, cols] = low

    def terms(k):
        d_part[k] = three_dots(u_high[k], u_low[k], x_high[k], x_low[k]).reshape(2, 16, 8, 256)
        peer_d(k).start()

    def peer_d(k):
        return remote(d_part.at[k, 1 - core], d_peer.at[k], c_ssem.at[k, 0], c_rsem.at[k, 0], sibling)

    def peer_rows(k, i):
        m = lax.rem(place + 1 + i, 8)
        return remote(y.at[k, m, 1 - core], y_peer.at[k, m], m_ssem.at[k, i], m_rsem.at[k, i], sibling)

    def rows_to_peer(k, i):
        rows_of_y(k, lax.rem(place + 1 + i, 8))
        peer_rows(k, i).start()

    def rows_to_chip(k, i):
        m = lax.rem(place + 1 + i, 8)
        peer_rows(k, i).wait()
        y_send[k, m] = y[k, m, core] + y_peer[k, m]

        @pl.when(i < 7)
        def _():
            chip_y(k, i + 1).start()

        @pl.when(i == 7)
        def _():
            y_recv[k, place] = y_send[k, place]

    def plane_d(k, step):
        to = (spot + step) % 16
        return remote(d_send.at[k, to], d_recv.at[k, spot], d_ssem.at[k, step], d_rsem.at[k, step], plane(step))

    def chip_y(k, step):
        to = (place + step) % 8
        return remote(y_send.at[k, to], y_recv.at[k, place], y_ssem.at[k, step], y_rsem.at[k, step], chip(step))

    def round_z(step):
        return remote(d_ring.at[z], d_ring.at[z], r_ssem.at[step], r_rsem.at[step], ring(step))

    def gather(step):
        mine = d_out.at[:, core, spot]
        return remote(mine, mine, g_ssem.at[step], g_rsem.at[step], plane(step))

    def peer_out():
        mine = d_out.at[:, core]
        return remote(mine, mine, c_ssem.at[0, 2], c_rsem.at[0, 2], sibling)

    def d_to_plane(k):
        peer_d(k).wait()
        d_send[k] = d_part[k, core] + d_peer[k]
        for step in range(1, 16):
            plane_d(k, step).start()
        d_recv[k, spot] = d_send[k, spot]

    def d_to_ring():
        for k in range(2):
            for step in range(1, 16):
                plane_d(k, step).wait()
            total = d_recv[k, 0]
            for i in range(1, 16):
                total = total + d_recv[k, i]
            d_ring[z, k] = total
        for step in range(1, RING):
            round_z(step).start()

    def d_to_gather():
        for step in range(1, RING):
            round_z(step).wait()
        for k in range(2):
            total = d_ring[0, k]
            for i in range(1, RING):
                total = total + d_ring[i, k]
            d_out[k, core, spot] = total
        for step in range(1, 16):
            gather(step).start()

    def sum_y(k):
        for step in range(1, 8):
            chip_y(k, step).wait()
        total = y_recv[k, 0]
        for i in range(1, 8):
            total = total + y_recv[k, i]
        slot = lax.div(q * 80, 128)
        rows = q * 80 + lax.broadcasted_iota(jnp.int32, (80, 256), 0)
        after = live_own[k * 10 + jnp.minimum(slot + 1, 9), 0:1]
        y_out[k] = -total * jnp.where(rows < slot * 128 + 128, live_own[k * 10 + slot, 0:1], after)

    load_a.wait()
    begin = jnp.where(hops == 0, STEPS, max(HALF, 26))
    begin_last = HALF + SUBS + SLACK

    def stream(t, carry):
        @pl.when(t < STEPS)
        def _():
            event(0, t)
            event(1, t)

        @pl.when(injects & (t < STEPS // 2 - LEAD))
        def _():
            entry_copy(t + LEAD).start()

        @pl.when(t < 20)
        def _():
            split_a(t)
            split_own(t)

        work = t - begin

        @pl.when((work >= 0) & (work < 5))
        def _():
            for i in range(2):
                take_block(0, work * 2 + i)

        @pl.when(work == 5)
        def _():
            terms(0)

        @pl.when((work >= 6) & (work < 14))
        def _():
            rows_to_peer(0, work - 6)

        @pl.when((work >= 6 + APART) & (work < 14 + APART))
        def _():
            rows_to_chip(0, work - 6 - APART)

        @pl.when(work == 5 + APART)
        def _():
            d_to_plane(0)

        @pl.when((t >= 20) & (t < 30))
        def _():
            left_product(t - 20)

        block = lax.div(t - begin_last, SUBS)

        @pl.when((t >= begin_last) & (block < 10) & (lax.rem(t - begin_last, SUBS) == 0))
        def _():
            take_block(1, block)

        return carry

    lax.fori_loop(0, STEPS + 14 + APART, stream, 0)

    terms(1)

    def last_rows(i, carry):
        @pl.when(i < 8)
        def _():
            rows_to_peer(1, i)

        @pl.when(i == 1)
        def _():
            d_to_plane(1)

        @pl.when(i >= 2)
        def _():
            rows_to_chip(1, i - 2)

        @pl.when(i == 6)
        def _():
            d_to_ring()

        return carry

    lax.fori_loop(0, 10, last_rows, 0)
    sum_y(0)
    def sent(s, carry):
        for way in range(2):
            _, up, down, to_x = roles(way, s)

            @pl.when(up)
            def _():
                z_copy(way, s, 1).wait_send()

            @pl.when(down)
            def _():
                z_copy(way, s, RING - 1).wait_send()

            @pl.when(to_x)
            def _():
                x_copy(way, s).wait_send()

        return carry

    lax.fori_loop(0, STEPS, sent, 0)

    def entered_all(j, carry):
        entry_copy(j).wait_send()
        return carry

    @pl.when(injects)
    def _():
        lax.fori_loop(0, STEPS // 2, entered_all, 0)

    d_to_gather()
    sum_y(1)
    for step in range(1, 16):
        gather(step).wait()
    peer_out().start()
    peer_out().wait()


def local(ancestor_inverse, factor_panel, structure, block_map, diag_inverse):
    dma = pltpu.SemaphoreType.DMA
    vmem = pltpu.VMEM
    columns, terms = pl.pallas_call(
        kernel,
        name="panel_product",
        out_shape=(jax.ShapeDtypeStruct((2, 80, 256), F32), jax.ShapeDtypeStruct((2, 2, 16, 8, 256), F32)),
        in_specs=[pl.BlockSpec(memory_space=pltpu.SMEM)] * 2 + [pl.BlockSpec(memory_space=pl.ANY)] * 2,
        out_specs=(pl.BlockSpec(memory_space=pltpu.VMEM),) * 2,
        scratch_shapes=[
            vmem((20, 8, 256), F32), vmem((20, 8, 256), F32), vmem((12800, 128), F32), vmem((1280, 1280), BF16), vmem((1280, 1280), BF16),
            vmem((2560, 256), F32), vmem((2, 256, 1280), BF16), vmem((2, 256, 1280), BF16),
            vmem((2, 256, 1280), BF16), vmem((2, 256, 1280), BF16),
            vmem((2560, 256), F32), vmem((2, 1280, 256), BF16), vmem((2, 1280, 256), BF16),
            vmem((2, 8, 2, 80, 256), F32), vmem((2, 8, 80, 256), F32), vmem((2, 8, 80, 256), F32),
            vmem((2, 8, 80, 256), F32),
            vmem((2, 2, 16, 8, 256), F32), vmem((2, 16, 8, 256), F32), vmem((2, 16, 8, 256), F32),
            vmem((2, 16, 8, 256), F32), vmem((RING, 2, 8, 256), F32),
            dma((3,)), dma((2, 2, STEPS)), dma((2, STEPS)), dma((2, STEPS)), dma((2, STEPS)), dma((2, STEPS)),
            dma((2, 3)), dma((2, 3)), dma((2, 8)), dma((2, 8)), dma((2, 16)), dma((2, 16)),
            dma((RING,)), dma((RING,)), dma((16,)), dma((16,)), dma((2, 8)), dma((2, 8)),
        ],
        compiler_params=pltpu.CompilerParams(collective_id=0, has_side_effects=True, vmem_limit_bytes=50 * 2**20),
    )(structure, block_map, ancestor_inverse.reshape(12800, 128), factor_panel.reshape(2560, 256))
    return columns[:, None, None], diag_inverse + terms.reshape(2, 256, 256)


def solution(mesh):
    in_specs = (
        P(None, "prow", None, None, "pcol", None),
        P(None, None, "prow", None, None),
        P(),
        P(),
        P(),
    )
    out_specs = (P(None, "prow", "pcol", None, None), P())
    return jax.shard_map(local, mesh=mesh, in_specs=in_specs, out_specs=out_specs, check_vma=False)
```

```python
import functools

import jax
import jax.numpy as jnp
from jax import lax
from jax.experimental import pallas as pl
from jax.experimental.pallas import tpu as pltpu
from jax.sharding import PartitionSpec as P

MESH = pl.DeviceIdType.MESH
F32 = jnp.float32
BF16 = jnp.bfloat16

RING = 8
SUBS = 2
ROWS = 64 // SUBS
STEPS = 2 * 10 * SUBS
PERIOD = 2
APART = 16
LEAD = 8
SLACK = 4
HALF = STEPS // 2


def split(value):
    high = value.astype(BF16)
    return high, (value - high.astype(F32)).astype(BF16)


def three_dots(a_high, a_low, b_high, b_low):
    dot = functools.partial(jnp.dot, preferred_element_type=F32)
    return dot(a_high, b_high) + (dot(a_high, b_low) + dot(a_low, b_high))


def kernel(
    structure, block_map, a_hbm, panel_hbm,
    y_out, d_out,
    live_own, live_col, a_raw, a_high, a_low, own, own_high, own_low, u_high, u_low, x, x_high, x_low,
    y, y_peer, y_send, y_recv, d_part, d_peer, d_send, d_recv, d_ring,
    load_sem, z_ssem, z_rsem, x_ssem, x_rsem, i_ssem, c_ssem, c_rsem, y_ssem, y_rsem, d_ssem, d_rsem,
    r_ssem, r_rsem, g_ssem, g_rsem, m_ssem, m_rsem,
):
    p = lax.axis_index("prow")
    q = lax.axis_index("pcol")
    half = p // RING
    z = p % RING
    place = q // 2
    core = q % 2
    root_half = q // RING
    hops = (z - q % RING + RING) % RING
    on_root = half == root_half

    spot = half * 8 + place
    across = ((1 - half) * RING + z, q)
    sibling = (p, place * 2 + 1 - core)

    def ring(step):
        return (half * RING + (z + step) % RING, q)

    def chip(step):
        return (p, ((place + step) % 8) * 2 + core)

    def plane(step):
        to = (spot + step) % 16
        return ((to // 8) * RING + z, (to % 8) * 2 + core)

    row_place = p // 2
    turn = (place // 2 - row_place // 2 + 4) % 4
    injects = (place % 2 != row_place % 2) & (core == p % 2)
    entry = ((1 - half) * RING + z, p)
    root = (root_half * RING + q % RING, q)

    def source(i):
        return (root[0], (((place // 2 + i) % 4) * 2 + 1 - place % 2) * 2 + core)

    load_own = pltpu.make_async_copy(panel_hbm, own, load_sem.at[0])
    load_own.start()
    load_root = pltpu.make_async_copy(panel_hbm, x, load_sem.at[1])

    @pl.when(p == q)
    def _():
        load_root.start()

    load_a = pltpu.make_async_copy(a_hbm, a_raw, load_sem.at[2])
    load_a.start()

    barrier = pltpu.get_barrier_semaphore()
    partners = [sibling] + [ring(i) for i in range(1, RING)] + [plane(i) for i in range(1, 16)]
    for partner in partners:
        pl.semaphore_signal(barrier, inc=1, device_id=partner, device_id_type=MESH)
    entered = (hops == 0) & jnp.logical_not(on_root)

    @pl.when(entered)
    def _():
        for i in range(4):
            pl.semaphore_signal(barrier, inc=1, device_id=source(i), device_id_type=MESH)

    @pl.when(injects)
    def _():
        pl.semaphore_signal(barrier, inc=1, device_id=entry, device_id_type=MESH)

    lanes = lax.broadcasted_iota(jnp.int32, (1, 256), 1)

    def mark(b, live):
        return tuple(jnp.where(lanes == block_map[structure[k, b]], 1.0, live[k]) for k in range(2))

    live = lax.fori_loop(0, 120, mark, (jnp.zeros((1, 256), F32),) * 2)
    for k in range(2):
        for r in range(10):
            for ref, index in ((live_own, p), (live_col, q)):
                found = jnp.sum(jnp.where(lanes == r * 16 + index, live[k], 0.0), axis=1, keepdims=True)
                ref[k * 10 + r] = jnp.broadcast_to(found, (8, 256))

    extra = jnp.where(entered, 4, 0) + jnp.where(injects, 1, 0)
    pl.semaphore_wait(barrier, len(partners) + extra)

    @pl.when(p == q)
    def _():
        load_root.wait()

    def rows_of_chunk(way, s):
        row = lax.div(s, SUBS) * 128 + way * 64 + lax.rem(s, SUBS) * ROWS
        return pl.ds(pl.multiple_of(row, ROWS), ROWS)

    def chunk(way, s):
        return x.at[rows_of_chunk(way, s)]

    def z_copy(way, s, step):
        return pltpu.make_async_remote_copy(
            src_ref=chunk(way, s), dst_ref=chunk(way, s), send_sem=z_ssem.at[min(step - 1, 1), way, s],
            recv_sem=z_rsem.at[way, s], device_id=ring(step), device_id_type=MESH,
        )

    def x_copy(way, s):
        return pltpu.make_async_remote_copy(
            src_ref=chunk(way, s), dst_ref=chunk(way, s), send_sem=x_ssem.at[way, s], recv_sem=x_rsem.at[way, s],
            device_id=across, device_id_type=MESH,
        )

    def roles(way, s):
        kind = jnp.where(lax.rem(s, 8) == 7, 2, lax.rem(s, PERIOD))
        both = kind >= 2
        carries = both | (kind == jnp.where(on_root, 0, 1))
        up = carries & (hops < RING // 2)
        down = carries & ((hops == 0) | (hops > RING // 2 + 1))
        to_x = (hops != 0) & carries & jnp.logical_not(both)
        return carries, up, down, to_x

    def event(way, s):
        carries, up, down, to_x = roles(way, s)

        @pl.when((hops == 0) & jnp.logical_not(on_root))
        def _():
            x_copy(way, s).wait_recv()

        @pl.when((hops != 0) & carries)
        def _():
            z_copy(way, s, 1).wait_recv()

        @pl.when(up)
        def _():
            z_copy(way, s, 1).start()

        @pl.when(down)
        def _():
            z_copy(way, s, RING - 1).start()

        @pl.when(to_x)
        def _():
            x_copy(way, s).start()

    def i_copy(way, s):
        src = own.at[rows_of_chunk(way, s)]
        return pltpu.make_async_remote_copy(
            src_ref=src, dst_ref=chunk(way, s), send_sem=i_ssem.at[way, s], recv_sem=x_rsem.at[way, s],
            device_id=entry, device_id_type=MESH,
        )

    def entry_copy(j):
        way = lax.rem(turn, 2)
        return i_copy(way, 2 * j + lax.div(turn, 2))

    def inject(j, carry):
        entry_copy(j).start()
        return carry

    load_own.wait()

    @pl.when(injects)
    def _():
        lax.fori_loop(0, LEAD, inject, 0)

    def remote(src, dst, send, recv, device):
        return pltpu.make_async_remote_copy(
            src_ref=src, dst_ref=dst, send_sem=send, recv_sem=recv, device_id=device, device_id_type=MESH
        )

    def split_a(i):
        for col in range(10):
            high, low = split(a_raw[pl.ds(i * 640 + col, 64, stride=10), :])
            rows = pl.ds(pl.multiple_of(i * 64, 64), 64)
            a_high[rows, col * 128 : (col + 1) * 128] = high
            a_low[rows, col * 128 : (col + 1) * 128] = low

    def split_own(i):
        k, r = lax.div(i, 10), lax.rem(i, 10)
        rows = pl.ds(pl.multiple_of(r * 128, 128), 128)
        high, low = split((own[pl.ds(pl.multiple_of(i * 128, 128), 128)] * live_own[i, 0:1]).T)
        own_high[k, :, rows] = high
        own_low[k, :, rows] = low

    def arrived(s):
        for way in range(2):
            carries, _, _, _ = roles(way, s)

            @pl.when((hops != 0) & jnp.logical_not(carries))
            def _():
                x_copy(way, s).wait_recv()

    def take_block(k, r):
        for sub in range(SUBS):
            arrived((k * 10 + r) * SUBS + sub)
        rows = pl.ds(pl.multiple_of(r * 128, 128), 128)
        high, low = split(x[pl.ds(pl.multiple_of((k * 10 + r) * 128, 128), 128)] * live_col[k * 10 + r, 0:1])
        x_high[k, rows] = high
        x_low[k, rows] = low

    def rows_of_y(k, m):
        rows = pl.ds(pl.multiple_of(m * 160, 32), 160)
        part = three_dots(a_high[rows], a_low[rows], x_high[k], x_low[k])
        y[k, m] = part.reshape(2, 80, 256)

    def left_product(i):
        k = lax.div(i, 5)
        cols = pl.ds(pl.multiple_of(lax.rem(i, 5) * 256, 256), 256)
        high, low = split(three_dots(own_high[k], own_low[k], a_high[:, cols], a_low[:, cols]))
        u_high[k, :, cols] = high
        u_low[k, :, cols] = low

    def terms(k):
        d_part[k] = three_dots(u_high[k], u_low[k], x_high[k], x_low[k]).reshape(2, 16, 8, 256)
        peer_d(k).start()

    def peer_d(k):
        return remote(d_part.at[k, 1 - core], d_peer.at[k], c_ssem.at[k, 0], c_rsem.at[k, 0], sibling)

    def peer_rows(k, i):
        m = lax.rem(place + 1 + i, 8)
        return remote(y.at[k, m, 1 - core], y_peer.at[k, m], m_ssem.at[k, i], m_rsem.at[k, i], sibling)

    def rows_to_peer(k, i):
        rows_of_y(k, lax.rem(place + 1 + i, 8))
        peer_rows(k, i).start()

    def rows_to_chip(k, i):
        m = lax.rem(place + 1 + i, 8)
        peer_rows(k, i).wait()
        y_send[k, m] = y[k, m, core] + y_peer[k, m]

        @pl.when(i < 7)
        def _():
            chip_y(k, i + 1).start()

        @pl.when(i == 7)
        def _():
            y_recv[k, place] = y_send[k, place]

    def plane_d(k, step):
        to = (spot + step) % 16
        return remote(d_send.at[k, to], d_recv.at[k, spot], d_ssem.at[k, step], d_rsem.at[k, step], plane(step))

    def chip_y(k, step):
        to = (place + step) % 8
        return remote(y_send.at[k, to], y_recv.at[k, place], y_ssem.at[k, step], y_rsem.at[k, step], chip(step))

    def round_z(step):
        return remote(d_ring.at[z], d_ring.at[z], r_ssem.at[step], r_rsem.at[step], ring(step))

    def gather(step):
        mine = d_out.at[:, core, spot]
        return remote(mine, mine, g_ssem.at[step], g_rsem.at[step], plane(step))

    def peer_out():
        mine = d_out.at[:, core]
        return remote(mine, mine, c_ssem.at[0, 2], c_rsem.at[0, 2], sibling)

    def d_to_plane(k):
        peer_d(k).wait()
        d_send[k] = d_part[k, core] + d_peer[k]
        for step in range(1, 16):
            plane_d(k, step).start()
        d_recv[k, spot] = d_send[k, spot]

    def d_to_ring():
        for k in range(2):
            for step in range(1, 16):
                plane_d(k, step).wait()
            total = d_recv[k, 0]
            for i in range(1, 16):
                total = total + d_recv[k, i]
            d_ring[z, k] = total
        for step in range(1, RING):
            round_z(step).start()

    def d_to_gather():
        for step in range(1, RING):
            round_z(step).wait()
        for k in range(2):
            total = d_ring[0, k]
            for i in range(1, RING):
                total = total + d_ring[i, k]
            d_out[k, core, spot] = total
        for step in range(1, 16):
            gather(step).start()

    def sum_y(k):
        for step in range(1, 8):
            chip_y(k, step).wait()
        total = y_recv[k, 0]
        for i in range(1, 8):
            total = total + y_recv[k, i]
        slot = lax.div(q * 80, 128)
        rows = q * 80 + lax.broadcasted_iota(jnp.int32, (80, 256), 0)
        after = live_own[k * 10 + jnp.minimum(slot + 1, 9), 0:1]
        y_out[k] = -total * jnp.where(rows < slot * 128 + 128, live_own[k * 10 + slot, 0:1], after)

    load_a.wait()
    begin = jnp.where(hops == 0, STEPS, max(HALF, 26))
    begin_last = HALF + SUBS + SLACK

    def stream(t, carry):
        @pl.when(t < STEPS)
        def _():
            event(0, t)
            event(1, t)

        @pl.when(injects & (t < STEPS // 2 - LEAD))
        def _():
            entry_copy(t + LEAD).start()

        @pl.when(t < 20)
        def _():
            split_a(t)
            split_own(t)

        work = t - begin

        @pl.when((work >= 0) & (work < 5))
        def _():
            for i in range(2):
                take_block(0, work * 2 + i)

        @pl.when(work == 5)
        def _():
            terms(0)

        @pl.when((work >= 6) & (work < 14))
        def _():
            rows_to_peer(0, work - 6)

        @pl.when((work >= 6 + APART) & (work < 14 + APART))
        def _():
            rows_to_chip(0, work - 6 - APART)

        @pl.when(work == 5 + APART)
        def _():
            d_to_plane(0)

        @pl.when((t >= 20) & (t < 30))
        def _():
            left_product(t - 20)

        block = lax.div(t - begin_last, SUBS)

        @pl.when((t >= begin_last) & (block < 10) & (lax.rem(t - begin_last, SUBS) == 0))
        def _():
            take_block(1, block)

        return carry

    lax.fori_loop(0, STEPS + 14 + APART, stream, 0)

    terms(1)

    def last_rows(i, carry):
        @pl.when(i < 8)
        def _():
            rows_to_peer(1, i)

        @pl.when(i == 1)
        def _():
            d_to_plane(1)

        @pl.when(i >= 2)
        def _():
            rows_to_chip(1, i - 2)

        @pl.when(i == 6)
        def _():
            d_to_ring()

        return carry

    lax.fori_loop(0, 10, last_rows, 0)
    sum_y(0)
    def sent(s, carry):
        for way in range(2):
            _, up, down, to_x = roles(way, s)

            @pl.when(up)
            def _():
                z_copy(way, s, 1).wait_send()

            @pl.when(down)
            def _():
                z_copy(way, s, RING - 1).wait_send()

            @pl.when(to_x)
            def _():
                x_copy(way, s).wait_send()

        return carry

    lax.fori_loop(0, STEPS, sent, 0)

    def entered_all(j, carry):
        entry_copy(j).wait_send()
        return carry

    @pl.when(injects)
    def _():
        lax.fori_loop(0, STEPS // 2, entered_all, 0)

    d_to_gather()
    sum_y(1)
    for step in range(1, 16):
        gather(step).wait()
    peer_out().start()
    peer_out().wait()


def local(ancestor_inverse, factor_panel, structure, block_map, diag_inverse):
    dma = pltpu.SemaphoreType.DMA
    vmem = pltpu.VMEM
    columns, terms = pl.pallas_call(
        kernel,
        name="panel_product",
        out_shape=(jax.ShapeDtypeStruct((2, 80, 256), F32), jax.ShapeDtypeStruct((2, 2, 16, 8, 256), F32)),
        in_specs=[pl.BlockSpec(memory_space=pltpu.SMEM)] * 2 + [pl.BlockSpec(memory_space=pl.ANY)] * 2,
        out_specs=(pl.BlockSpec(memory_space=pltpu.VMEM),) * 2,
        scratch_shapes=[
            vmem((20, 8, 256), F32), vmem((20, 8, 256), F32), vmem((12800, 128), F32), vmem((1280, 1280), BF16), vmem((1280, 1280), BF16),
            vmem((2560, 256), F32), vmem((2, 256, 1280), BF16), vmem((2, 256, 1280), BF16),
            vmem((2, 256, 1280), BF16), vmem((2, 256, 1280), BF16),
            vmem((2560, 256), F32), vmem((2, 1280, 256), BF16), vmem((2, 1280, 256), BF16),
            vmem((2, 8, 2, 80, 256), F32), vmem((2, 8, 80, 256), F32), vmem((2, 8, 80, 256), F32),
            vmem((2, 8, 80, 256), F32),
            vmem((2, 2, 16, 8, 256), F32), vmem((2, 16, 8, 256), F32), vmem((2, 16, 8, 256), F32),
            vmem((2, 16, 8, 256), F32), vmem((RING, 2, 8, 256), F32),
            dma((3,)), dma((2, 2, STEPS)), dma((2, STEPS)), dma((2, STEPS)), dma((2, STEPS)), dma((2, STEPS)),
            dma((2, 3)), dma((2, 3)), dma((2, 8)), dma((2, 8)), dma((2, 16)), dma((2, 16)),
            dma((RING,)), dma((RING,)), dma((16,)), dma((16,)), dma((2, 8)), dma((2, 8)),
        ],
        compiler_params=pltpu.CompilerParams(collective_id=0, has_side_effects=True, vmem_limit_bytes=50 * 2**20),
    )(structure, block_map, ancestor_inverse.reshape(12800, 128), factor_panel.reshape(2560, 256))
    return columns[:, None, None], diag_inverse + terms.reshape(2, 256, 256)


def solution(mesh):
    in_specs = (
        P(None, "prow", None, None, "pcol", None),
        P(None, None, "prow", None, None),
        P(),
        P(),
        P(),
    )
    out_specs = (P(None, "prow", "pcol", None, None), P())
    return jax.shard_map(local, mesh=mesh, in_specs=in_specs, out_specs=out_specs, check_vma=False)
```
